256 devices in a mesh: dp: 16 (over z, core), tensor: 16 (over y, x).
Axes of the slice: x: 4, y: 4, z: 8, core: 2. Of those that a mesh axis runs over, the one named last changes fastest.
Arguments:
- out_grad: bfloat16 [16384, 4096], P('dp'), may hold values from -6 to 6
- gate_pre: bfloat16 [16384, 11008], P('dp', 'tensor'), may hold values from -6 to 6
- up_pre: bfloat16 [16384, 11008], P('dp', 'tensor'), may hold values from -6 to 6
- down_weight: bfloat16 [11008, 4096], P('tensor'), may hold values from -0.09375 to 0.09375
- proj_hidden: bfloat16 [11008, 64], P('tensor'), may hold values from -0.0546875 to 0.0546875
- proj_out: bfloat16 [4096, 64], replicated, may hold values from -0.09375 to 0.09375
- example_ids: int32 [16384], P('dp'), may hold values from 0 to 63, never falling along the last dimension, each value on 1 to 512 neighbouring positions
- queries: bfloat16 [4096, 4096], P('dp', 'tensor'), may hold values from -0.01171875 to 0.01171875
Outputs:
- gate_grad: bfloat16 [16384, 11008], P('dp', 'tensor')
- up_grad: bfloat16 [16384, 11008], P('dp', 'tensor')
- scores: float32 [64, 4096], P('tensor', 'dp')
The draws below stay inside these ranges and needn't reach their ends.
Inputs may be any that keep to these rules, and one draw needn't show every extreme that they name: `example_ids`: example numbers never fall along the tokens; each example holds 1 to 512 tokens and one holds exactly that many.
All inputs are finite; a program needn't handle non-finite values.
Results may differ from the reference program's by a relative error of at most 0.0049.
Values may be sent and summed in bfloat16 or wider, within the bound.
No kernel may reach another device: no remote copies, remote signals or barrier semaphores. Data moves between devices by JAX's collectives and lax.ppermute only.
A program may use at most 64 MiB of HBM per device.

```python
import math
import jax
import jax.numpy as jnp
import numpy as np
from jax import lax

D = 4096
FF = 11008
R = 64
TOK_DEV = 1024
EX_DEV = 4
TOKENS = 16384
EXAMPLES = 64
QUERIES = 4096


def block_levels(stream_key, extent, split, smallest, largest):
    loudness, own = 1.0, jax.random.fold_in(stream_key, 6)
    for position, shards_of in split:
        draws = jnp.exp(jax.random.uniform(jax.random.fold_in(own, position), (shards_of,), jnp.float32, smallest / len(split), largest / len(split)))
        loudness = loudness * jnp.repeat(draws, extent[position] // shards_of).reshape([-1 if axis == position else 1 for axis in range(len(extent))])
    return loudness


def length_profile(amount, total, reach, skew):
    loads = [(1 << 20) // math.isqrt(grade ** skew) + 1 for grade in range(2, amount + 1)]
    rest, given = total - reach - (amount - 1), [1] * (amount - 1)
    while rest > 0:
        candidates = [i for i in range(amount - 1) if given[i] < reach]
        mass, budget = sum([loads[i] for i in candidates]), rest
        for i in candidates:
            more = min(reach - given[i], max(1, budget * loads[i] // mass), rest)
            given[i] = given[i] + more
            rest = rest - more
    return np.array([reach] + given)


def uneven(rng, amount, total, most, slope):
    if amount == 2:
        one = jax.random.randint(rng, (), max(1, total - most), min(most, total - 1) + 1)
        return jnp.stack([one, total - one])
    lengths = jnp.asarray(length_profile(amount, total, most, slope), jnp.int32)
    pairs = (amount - 1) // 2
    giver, receiver = lengths[1:1 + 2 * pairs:2], lengths[2:2 + 2 * pairs:2]
    slack = jnp.minimum(giver - 1, most - receiver)
    passed = jax.random.randint(jax.random.fold_in(rng, 1), (pairs,), 0, 1 << 20) % (slack + 1)
    lengths = lengths.at[1:1 + 2 * pairs:2].set(giver - passed).at[2:2 + 2 * pairs:2].set(receiver + passed)
    return lengths[jax.random.permutation(jax.random.fold_in(rng, 2), amount)]


def gaussian(own_key, extent, width, reach, split=(), kind=jnp.bfloat16):
    values = jax.random.normal(own_key, extent, jnp.float32) * width
    if len(split) > 0:
        values = block_levels(own_key, extent, split, -0.22, 0.18) * values
    return jnp.clip(values, min=-reach, max=reach).astype(kind)


def setup_inputs(seed: int = 0) -> dict:
    splits = jax.random.split(jax.random.key(seed), 9)
    out_grad = gaussian(splits[0], (TOKENS, D), 1.0, 6.0, ((0, 16),))
    gate_pre = gaussian(splits[1], (TOKENS, FF), 1.0, 6.0, ((0, 16), (1, 16)))
    up_pre = gaussian(splits[2], (TOKENS, FF), 1.0, 6.0, ((0, 16), (1, 16)))
    down_weight = gaussian(splits[3], (FF, D), D ** -0.5, 0.09375, ((0, 16),))
    proj_hidden = gaussian(splits[4], (FF, R), FF ** -0.5, 0.0546875, ((0, 16),))
    proj_out = gaussian(splits[5], (D, R), D ** -0.5, 0.09375)
    example_ids = jnp.searchsorted(jnp.cumsum(uneven(splits[6], EXAMPLES, TOKENS, 2 * TOK_DEV // EX_DEV, 1)), jnp.arange(TOKENS), side="right").astype(jnp.int32)
    queries = gaussian(splits[7], (QUERIES, R * R), (R * R * TOK_DEV // EX_DEV // 4) ** -0.5, 0.01171875, ((0, 16), (1, 16)))
    return {"out_grad": out_grad, "gate_pre": gate_pre, "up_pre": up_pre, "down_weight": down_weight, "proj_hidden": proj_hidden, "proj_out": proj_out, "example_ids": example_ids, "queries": queries}


def reference(out_grad, gate_pre, up_pre, down_weight, proj_hidden, proj_out, example_ids, queries):
    gate_val = gate_pre.astype(jnp.float32)
    up_val = up_pre.astype(jnp.float32)
    sigmoid_gate = jax.nn.sigmoid(gate_val)
    hidden = (gate_val * sigmoid_gate * up_val).astype(jnp.bfloat16)
    hidden_grad = jnp.dot(out_grad, down_weight.T, preferred_element_type=jnp.float32)
    up_grad = (hidden_grad * gate_val * sigmoid_gate).astype(jnp.bfloat16)
    gate_grad = (hidden_grad * up_val * sigmoid_gate * (1.0 + gate_val * (1.0 - sigmoid_gate))).astype(jnp.bfloat16)
    act_proj = jnp.dot(hidden, proj_hidden, preferred_element_type=jnp.float32)
    grad_proj = jnp.dot(out_grad, proj_out, preferred_element_type=jnp.float32)
    member = (example_ids[:, None] == jnp.arange(EXAMPLES, dtype=jnp.int32)[None, :]).astype(jnp.float32)
    weighted = (member[:, :, None] * act_proj[:, None, :]).reshape(TOKENS, EXAMPLES * R)
    per_example = lax.dot_general(weighted, grad_proj, (((0,), (0,)), ((), ())), precision=lax.Precision.HIGHEST)
    example_grads = per_example.reshape(EXAMPLES, R * R).astype(jnp.bfloat16)
    scores = lax.dot_general(example_grads, queries, (((1,), (1,)), ((), ())), preferred_element_type=jnp.float32)
    return gate_grad, up_grad, scores
```

```python
import functools
import jax
import jax.numpy as jnp
from jax import lax
from jax.experimental import pallas as pl
from jax.experimental.pallas import tpu as pltpu
from jax.sharding import PartitionSpec as P

F32 = jnp.float32
BF16 = jnp.bfloat16
EXAMPLES = 64
MAX_COPIES = 80
ACT_PARTS = ((0, 256), (256, 256), (512, 176))
LIMIT = 60 << 20
LAST_ROWS = ((192, 256), (448, 240))
FIRST = (
    True,
    ((0, 192),),
    (0, 1, 2, 3),
    (("grad", 1), ("grad", 2), ("value", 0), ("grad", 3)),
    (
        ((("grad", 1),), ((0, 1),), ()),
        ((("grad", 2), ("value", 0)), ((0, 2),), ()),
        ((("grad", 3),), ((0, 3),), (0,)),
    ),
)
SECOND = (
    False,
    LAST_ROWS,
    (0, 1, 2),
    (("grad", 1), ("weight", 1), ("value", 0), ("value", 1), ("grad", 2)),
    (
        ((("grad", 1),), ((0, 1),), ()),
        ((("weight", 1), ("value", 0)), ((1, 0), (1, 1)), ()),
        ((("value", 1), ("grad", 2)), ((0, 2), (1, 2)), (0, 1)),
    ),
)
THIRD = (
    False,
    LAST_ROWS,
    (3,),
    (("weight", 1), ("value", 0), ("value", 1)),
    (((("weight", 1), ("value", 0), ("value", 1)), ((1, 3),), (0, 1)),),
)
TOK_BLOCK = 256
NT = (((1,), (1,)), ((), ()))
HBM = pl.BlockSpec(memory_space=pltpu.HBM)
ANY = pl.BlockSpec(memory_space=pl.ANY)
VMEM = pl.BlockSpec(memory_space=pltpu.VMEM)
MIB = 1 << 20


def act_kernel(gate_ref, up_ref, proj_ref, out_ref, gates, ups, projs, sems):
    proj_copy = pltpu.make_async_copy(proj_ref, projs, sems.at[0])
    copies = []
    for index, (start, rows) in enumerate(ACT_PARTS):
        part = pl.ds(start, rows)
        copies.append((
            pltpu.make_async_copy(gate_ref.at[part], gates.at[part], sems.at[1 + 2 * index]),
            pltpu.make_async_copy(up_ref.at[part], ups.at[part], sems.at[2 + 2 * index]),
        ))
    for gate_copy, up_copy in copies[:1]:
        gate_copy.start()
        up_copy.start()
    proj_copy.start()
    for gate_copy, up_copy in copies[1:]:
        gate_copy.start()
        up_copy.start()
    act = None
    for (gate_copy, up_copy), (start, rows) in zip(copies, ACT_PARTS):
        gate_copy.wait()
        up_copy.wait()
        gate = gates[start:start + rows, :].astype(F32)
        up = ups[start:start + rows, :].astype(F32)
        hidden = (gate * jax.nn.sigmoid(gate) * up).astype(BF16)
        if act is None:
            proj_copy.wait()
        term = jnp.dot(projs[:, start:start + rows], hidden, preferred_element_type=F32)
        act = term if act is None else act + term
    for part in range(16):
        for block in range(8):
            out_ref[part, 4 * block:4 * block + 4, :] = act[
                4 * part:4 * part + 4, 128 * block:128 * block + 128
            ]


def act_parts(gate, up, proj):
    hidden_units, tokens = gate.shape
    ranks = proj.shape[0]
    return pl.pallas_call(
        act_kernel,
        in_specs=[HBM] * 3,
        out_specs=VMEM,
        out_shape=jax.ShapeDtypeStruct((16, 32, 128), F32),
        scratch_shapes=[
            pltpu.VMEM(gate.shape, BF16),
            pltpu.VMEM(gate.shape, BF16),
            pltpu.VMEM(proj.shape, BF16),
            pltpu.SemaphoreType.DMA((1 + 2 * len(ACT_PARTS),)),
        ],
        compiler_params=pltpu.CompilerParams(vmem_limit_bytes=LIMIT),
        cost_estimate=pl.CostEstimate(
            flops=2 * ranks * hidden_units * tokens,
            bytes_accessed=4 * hidden_units * tokens,
            transcendentals=hidden_units * tokens,
        ),
        name="act_parts",
    )(gate, up, proj)


def grads_kernel(plan, grad_ref, weight_ref, gate_ref, up_ref, *rest):
    first, row_parts, tok_parts, loads, blocks = plan
    if first:
        proj_ref, gate_out, up_out, order_out, proj_out = rest[:5]
        rank = proj_ref.shape[0]
    else:
        gate_out, up_out, order_out = rest[3:6]
        rank = 0
    grads, weights, gates, ups, gate_done, up_done, products, sems = rest[-8:]
    width = grads.shape[1]
    first_row, first_tok = row_parts[0][0], tok_parts[0]
    all_tokens = pl.ds(TOK_BLOCK * first_tok, TOK_BLOCK * len(tok_parts))
    sem = iter(range(MAX_COPIES))
    copies = {}

    def start(key, *pairs):
        for source, target in pairs:
            part = pltpu.make_async_copy(source, target, sems.at[next(sem)])
            part.start()
            copies.setdefault(key, []).append(part)

    def wait(*keys):
        for key in keys:
            for part in copies.pop(key):
                part.wait()

    def tokens(part):
        return pl.ds(TOK_BLOCK * part, TOK_BLOCK)

    def local_tokens(part):
        return pl.ds(TOK_BLOCK * (part - first_tok), TOK_BLOCK)

    def rows(part):
        return pl.ds(*row_parts[part])

    def local_rows(part):
        row, size = row_parts[part]
        return pl.ds(row - first_row, size)

    def load(kind, part, half=None):
        columns = pl.ds(0, width) if half is None else pl.ds(width // 2 * half, width // 2)
        key = (kind, part) if half is None else (kind, part, half)
        if kind == "grad":
            target = grads.at[local_tokens(part), columns]
            start(key, (grad_ref.at[tokens(part), columns], target))
        elif kind == "weight":
            row, size = row_parts[part]
            target = weights.at[pl.ds(rank + row - first_row, size), columns]
            start(key, (weight_ref.at[rows(part), columns], target))
        elif kind == "proj":
            start(key, (proj_ref.at[:, columns], weights.at[pl.ds(0, rank), columns]))
        else:
            place = (rows(part), all_tokens)
            start(
                key,
                (gate_ref.at[place], gates.at[local_rows(part), :]),
                (up_ref.at[place], ups.at[local_rows(part), :]),
            )

    def multiply(row_part, tok_part, columns):
        row, size = row_parts[row_part]
        area = pl.ds(rank + row - first_row, size) if row_part else pl.ds(0, rank + size)
        return lax.dot_general(
            weights[area, columns],
            grads[local_tokens(tok_part), columns],
            NT,
            preferred_element_type=F32,
        )

    def keep(row_part, tok_part, product):
        tok = local_tokens(tok_part)
        if first and row_part == 0:
            projected = product[:rank]
            high = projected.astype(BF16)
            proj_out[:rank, tok] = high
            proj_out[rank:, tok] = (projected - high.astype(F32)).astype(BF16)
            product = product[rank:]
        products[local_rows(row_part), tok] = product

    def finish(row_part, tok_part):
        here = (local_rows(row_part), local_tokens(tok_part))
        gate = gates[here].astype(F32)
        sig = jax.nn.sigmoid(gate)
        scaled = products[here] * sig
        up_done[here] = (scaled * gate).astype(BF16)
        gate_done[here] = (
            scaled * ups[here].astype(F32) * (1.0 + gate * (1.0 - sig))
        ).astype(BF16)

    def store(row_part):
        place = (rows(row_part), all_tokens)
        here = local_rows(row_part)
        start(
            "out",
            (gate_done.at[here, :], gate_out.at[place]),
            (up_done.at[here, :], up_out.at[place]),
        )

    kinds = [("grad", first_tok), ("weight", 0)] + [("proj", 0)] * first
    for half in range(2):
        for kind, part in kinds:
            load(kind, part, half)
    for kind, part in loads:
        load(kind, part)
    product = None
    for half in range(2):
        wait(*((*key, half) for key in kinds))
        term = multiply(0, first_tok, pl.ds(width // 2 * half, width // 2))
        product = term if product is None else product + term
    keep(0, first_tok, product)
    pending = [(0, first_tok)]
    for needs, tiles, rows_done in blocks:
        wait(*needs)
        for tile in tiles:
            keep(*tile, multiply(*tile, slice(None)))
            pending.append(tile)
            while len(pending) > 1 and ("value", pending[0][0]) not in copies:
                finish(*pending.pop(0))
        if rows_done:
            while pending:
                finish(*pending.pop(0))
        for row_part in rows_done:
            store(row_part)
    wait("out")


def grads_call(plan, grad, weight, gate, up, proj=None, before=None, after=None):
    first, row_parts, tok_parts = plan[:3]
    width = grad.shape[1]
    rows = sum(size for _, size in row_parts)
    tokens = TOK_BLOCK * len(tok_parts)
    in_specs = [HBM] * 4
    out_specs = [HBM, HBM, HBM]
    out_shape = [jax.ShapeDtypeStruct(gate.shape, BF16)] * 2 + [jax.ShapeDtypeStruct((8, 128), F32)]
    if first:
        in_specs.append(HBM)
        out_specs.append(VMEM)
        out_shape.append(jax.ShapeDtypeStruct((2 * proj.shape[0], tokens), BF16))
        extra, aliases = (proj,), {}
    else:
        in_specs += [HBM, HBM, ANY]
        extra, aliases = (*before, after), {4: 0, 5: 1}
    return pl.pallas_call(
        functools.partial(grads_kernel, plan),
        in_specs=in_specs,
        out_specs=out_specs,
        out_shape=out_shape,
        scratch_shapes=[
            pltpu.VMEM((tokens, width), BF16),
            pltpu.VMEM((rows + 64 * first, width), BF16),
            *[pltpu.VMEM((rows, tokens), BF16)] * 4,
            pltpu.VMEM((rows, tokens), F32),
            pltpu.SemaphoreType.DMA((MAX_COPIES,)),
        ],
        input_output_aliases=aliases,
        compiler_params=pltpu.CompilerParams(vmem_limit_bytes=LIMIT),
        cost_estimate=pl.CostEstimate(
            flops=2 * rows * tokens * width,
            bytes_accessed=2 * (tokens + rows) * width + 8 * rows * tokens,
            transcendentals=rows * tokens,
        ),
        name="grads_%d_%d" % (row_parts[0][0], tok_parts[0]),
    )(grad, weight, gate, up, *extra)


def example_kernel(parts_ref, ids_ref, proj_ref, out_ref):
    act = parts_ref[0]
    for part in range(1, 16):
        act = act + parts_ref[part]
    example = lax.broadcasted_iota(jnp.int32, (EXAMPLES, 128), 0)
    members = [ids_ref[block:block + 1, :] == example for block in range(8)]
    projected = proj_ref[...]
    for rank in range(4):
        weighted = jnp.concatenate(
            [
                jnp.where(members[block], act[4 * block + rank:4 * block + rank + 1, :], 0.0)
                for block in range(8)
            ],
            axis=1,
        )
        high = weighted.astype(BF16)
        low = (weighted - high.astype(F32)).astype(BF16)
        first = lax.dot_general(high, projected, NT, preferred_element_type=F32)
        second = lax.dot_general(low, projected[:64], NT, preferred_element_type=F32)
        out_ref[:, 64 * rank:64 * rank + 64] = first[:, :64] + (first[:, 64:] + second)


def example_terms(parts, ids, proj):
    return pl.pallas_call(
        example_kernel,
        out_shape=jax.ShapeDtypeStruct((EXAMPLES, 256), F32),
        compiler_params=pltpu.CompilerParams(vmem_limit_bytes=16 * MIB),
        cost_estimate=pl.CostEstimate(flops=100_000_000, bytes_accessed=700_000, transcendentals=0),
        name="example_terms",
    )(parts, ids, proj)


def score_kernel(terms_ref, queries_ref, _order, out_ref):
    total = terms_ref[0].astype(F32)
    for part in range(1, 8):
        total = total + terms_ref[part].astype(F32)
    scores = lax.dot_general(
        total.astype(BF16), queries_ref[...], NT, preferred_element_type=F32
    )
    for part in range(16):
        for half in range(2):
            out_ref[part, 4 * half:4 * half + 4, :] = scores[
                4 * part:4 * part + 4, 128 * half:128 * half + 128
            ]


def score_parts(terms, queries, order):
    return pl.pallas_call(
        score_kernel,
        in_specs=[VMEM, VMEM, HBM],
        out_specs=VMEM,
        out_shape=jax.ShapeDtypeStruct((16, 8, 128), F32),
        compiler_params=pltpu.CompilerParams(vmem_limit_bytes=16 * MIB),
        cost_estimate=pl.CostEstimate(flops=10_000_000, bytes_accessed=500_000, transcendentals=0),
        name="score_parts",
    )(terms, queries, order)


def final_kernel(parts_ref, _order, out_ref):
    total = parts_ref[0]
    for part in range(1, 16):
        total = total + parts_ref[part]
    out_ref[:, :128] = total[:4]
    out_ref[:, 128:] = total[4:]


def final_sum(parts, order):
    return pl.pallas_call(
        final_kernel,
        in_specs=[VMEM, HBM],
        out_specs=VMEM,
        out_shape=jax.ShapeDtypeStruct((4, 256), F32),
        compiler_params=pltpu.CompilerParams(vmem_limit_bytes=16 * MIB),
        cost_estimate=pl.CostEstimate(flops=100_000, bytes_accessed=70_000, transcendentals=0),
        name="final_sum",
    )(parts, order)


def on_device(out_grad, gate_pre, up_pre, down_weight, proj_hidden, proj_out, example_ids, queries):
    gate, up = gate_pre.T, up_pre.T
    exchange = functools.partial(
        lax.all_to_all, axis_name="tensor", split_axis=0, concat_axis=0, tiled=True
    )
    sent = act_parts(gate, up, proj_hidden.T)
    parts = exchange(sent)
    gate_grad, up_grad, _, projected = grads_call(
        FIRST, out_grad, down_weight, gate, up, proj=proj_out.T
    )
    terms = example_terms(parts, example_ids.reshape(8, 128), projected)
    other = lax.ppermute(terms, "dp", [(i, i ^ 1) for i in range(16)])
    pair = (terms + other).astype(BF16)
    pairs = jnp.broadcast_to(pair[None], (8, *pair.shape))
    chips = [[2 * z + core for z in range(8)] for core in range(2)]
    all_terms = lax.all_to_all(
        pairs, "dp", split_axis=0, concat_axis=0, tiled=True, axis_index_groups=chips
    )
    gate_grad, up_grad, order = grads_call(
        SECOND, out_grad, down_weight, gate, up, before=(gate_grad, up_grad), after=pair
    )
    scores = score_parts(all_terms, queries, order)
    score_terms = exchange(scores)
    gate_grad, up_grad, order = grads_call(
        THIRD, out_grad, down_weight, gate, up, before=(gate_grad, up_grad), after=scores
    )
    return gate_grad.T, up_grad.T, final_sum(score_terms, order)


def solution(mesh):
    in_specs = (
        P("dp", None),
        P("dp", "tensor"),
        P("dp", "tensor"),
        P("tensor", None),
        P("tensor", None),
        P(),
        P("dp"),
        P("dp", "tensor"),
    )
    out_specs = (P("dp", "tensor"), P("dp", "tensor"), P("tensor", "dp"))
    return jax.shard_map(
        on_device, mesh=mesh, in_specs=in_specs, out_specs=out_specs, check_vma=False
    )
```

```python
import functools
import jax
import jax.numpy as jnp
from jax import lax
from jax.experimental import pallas as pl
from jax.experimental.pallas import tpu as pltpu
from jax.sharding import PartitionSpec as P

F32 = jnp.float32
BF16 = jnp.bfloat16
EXAMPLES = 64
MAX_COPIES = 80
ACT_PARTS = ((0, 256), (256, 256), (512, 176))
LIMIT = 60 << 20
LAST_ROWS = ((192, 256), (448, 240))
FIRST = (
    True,
    ((0, 192),),
    (0, 1, 2, 3),
    (("grad", 0), ("weight", 0), ("proj", 0), ("grad", 1), ("value", 0), ("grad", 2), ("grad", 3)),
    (
        ((("grad", 0), ("weight", 0), ("proj", 0), ("grad", 1)), ((0, 0), (0, 1)), ()),
        ((("grad", 2), ("grad", 3), ("value", 0)), ((0, 2), (0, 3)), (0,)),
    ),
)
SECOND = (
    False,
    LAST_ROWS,
    (0, 1, 2),
    (
        ("grad", 0), ("weight", 0), ("grad", 1), ("weight", 1), ("value", 0), ("grad", 2),
        ("value", 1),
    ),
    (
        ((("grad", 0), ("weight", 0), ("grad", 1)), ((0, 0), (0, 1)), ()),
        (
            (("weight", 1), ("value", 0), ("value", 1), ("grad", 2)),
            ((1, 0), (1, 1), (0, 2), (1, 2)),
            (0, 1),
        ),
    ),
)
THIRD = (
    False,
    LAST_ROWS,
    (3,),
    (("grad", 3), ("weight", 0), ("weight", 1), ("value", 0), ("value", 1)),
    (
        (
            (("grad", 3), ("weight", 0), ("weight", 1), ("value", 0), ("value", 1)),
            ((0, 3), (1, 3)),
            (0, 1),
        ),
    ),
)
TOK_BLOCK = 256
NT = (((1,), (1,)), ((), ()))
HBM = pl.BlockSpec(memory_space=pltpu.HBM)
ANY = pl.BlockSpec(memory_space=pl.ANY)
VMEM = pl.BlockSpec(memory_space=pltpu.VMEM)
MIB = 1 << 20


def act_kernel(gate_ref, up_ref, proj_ref, out_ref, gates, ups, projs, sems):
    proj_copy = pltpu.make_async_copy(proj_ref, projs, sems.at[0])
    copies = []
    for index, (start, rows) in enumerate(ACT_PARTS):
        part = pl.ds(start, rows)
        copies.append((
            pltpu.make_async_copy(gate_ref.at[part], gates.at[part], sems.at[1 + 2 * index]),
            pltpu.make_async_copy(up_ref.at[part], ups.at[part], sems.at[2 + 2 * index]),
        ))
    for gate_copy, up_copy in copies[:1]:
        gate_copy.start()
        up_copy.start()
    proj_copy.start()
    for gate_copy, up_copy in copies[1:]:
        gate_copy.start()
        up_copy.start()
    act = None
    for (gate_copy, up_copy), (start, rows) in zip(copies, ACT_PARTS):
        gate_copy.wait()
        up_copy.wait()
        gate = gates[start:start + rows, :].astype(F32)
        up = ups[start:start + rows, :].astype(F32)
        hidden = (gate * jax.nn.sigmoid(gate) * up).astype(BF16)
        if act is None:
            proj_copy.wait()
        term = jnp.dot(projs[:, start:start + rows], hidden, preferred_element_type=F32)
        act = term if act is None else act + term
    for part in range(16):
        for block in range(8):
            out_ref[part, 4 * block:4 * block + 4, :] = act[
                4 * part:4 * part + 4, 128 * block:128 * block + 128
            ]


def act_parts(gate, up, proj):
    hidden_units, tokens = gate.shape
    ranks = proj.shape[0]
    return pl.pallas_call(
        act_kernel,
        in_specs=[HBM] * 3,
        out_specs=VMEM,
        out_shape=jax.ShapeDtypeStruct((16, 32, 128), F32),
        scratch_shapes=[
            pltpu.VMEM(gate.shape, BF16),
            pltpu.VMEM(gate.shape, BF16),
            pltpu.VMEM(proj.shape, BF16),
            pltpu.SemaphoreType.DMA((1 + 2 * len(ACT_PARTS),)),
        ],
        compiler_params=pltpu.CompilerParams(vmem_limit_bytes=LIMIT),
        cost_estimate=pl.CostEstimate(
            flops=2 * ranks * hidden_units * tokens,
            bytes_accessed=4 * hidden_units * tokens,
            transcendentals=hidden_units * tokens,
        ),
        name="act_parts",
    )(gate, up, proj)


def grads_kernel(plan, grad_ref, weight_ref, gate_ref, up_ref, *rest):
    first, row_parts, tok_parts, loads, blocks = plan
    if first:
        proj_ref, gate_out, up_out, order_out, proj_out = rest[:5]
        rank = proj_ref.shape[0]
    else:
        gate_out, up_out, order_out = rest[3:6]
        rank = 0
    grads, weights, gates, ups, gate_done, up_done, products, sems = rest[-8:]
    width = grads.shape[1]
    first_row, first_tok = row_parts[0][0], tok_parts[0]
    all_tokens = pl.ds(TOK_BLOCK * first_tok, TOK_BLOCK * len(tok_parts))
    sem = iter(range(MAX_COPIES))
    copies = {}

    def start(key, *pairs):
        for source, target in pairs:
            part = pltpu.make_async_copy(source, target, sems.at[next(sem)])
            part.start()
            copies.setdefault(key, []).append(part)

    def wait(*keys):
        for key in keys:
            for part in copies.pop(key):
                part.wait()

    def tokens(part):
        return pl.ds(TOK_BLOCK * part, TOK_BLOCK)

    def local_tokens(part):
        return pl.ds(TOK_BLOCK * (part - first_tok), TOK_BLOCK)

    def rows(part):
        return pl.ds(*row_parts[part])

    def local_rows(part):
        row, size = row_parts[part]
        return pl.ds(row - first_row, size)

    def load(kind, part):
        key = (kind, part)
        if kind == "grad":
            start(key, (grad_ref.at[tokens(part), :], grads.at[local_tokens(part), :]))
        elif kind == "weight":
            row, size = row_parts[part]
            target = weights.at[pl.ds(rank + row - first_row, size), :]
            start(key, (weight_ref.at[rows(part), :], target))
        elif kind == "proj":
            start(key, (proj_ref, weights.at[pl.ds(0, rank), :]))
        else:
            place = (rows(part), all_tokens)
            start(
                key,
                (gate_ref.at[place], gates.at[local_rows(part), :]),
                (up_ref.at[place], ups.at[local_rows(part), :]),
            )

    def multiply(row_part, tok_part):
        row, size = row_parts[row_part]
        area = pl.ds(rank + row - first_row, size) if row_part else pl.ds(0, rank + size)
        return lax.dot_general(
            weights[area, :],
            grads[local_tokens(tok_part), :],
            NT,
            preferred_element_type=F32,
        )

    def keep(row_part, tok_part, product):
        tok = local_tokens(tok_part)
        if first and row_part == 0:
            projected = product[:rank]
            high = projected.astype(BF16)
            proj_out[:rank, tok] = high
            proj_out[rank:, tok] = (projected - high.astype(F32)).astype(BF16)
            product = product[rank:]
        products[local_rows(row_part), tok] = product

    def finish(row_part, tok_part):
        here = (local_rows(row_part), local_tokens(tok_part))
        gate = gates[here].astype(F32)
        sig = jax.nn.sigmoid(gate)
        scaled = products[here] * sig
        up_done[here] = (scaled * gate).astype(BF16)
        gate_done[here] = (
            scaled * ups[here].astype(F32) * (1.0 + gate * (1.0 - sig))
        ).astype(BF16)

    def store(row_part):
        place = (rows(row_part), all_tokens)
        here = local_rows(row_part)
        start(
            "out",
            (gate_done.at[here, :], gate_out.at[place]),
            (up_done.at[here, :], up_out.at[place]),
        )

    for kind, part in loads:
        load(kind, part)
    pending = []
    for needs, tiles, rows_done in blocks:
        wait(*needs)
        for tile in tiles:
            keep(*tile, multiply(*tile))
            pending.append(tile)
            while len(pending) > 1 and ("value", pending[0][0]) not in copies:
                finish(*pending.pop(0))
        if rows_done:
            while pending:
                finish(*pending.pop(0))
        for row_part in rows_done:
            store(row_part)
    wait("out")


def grads_call(plan, grad, weight, gate, up, proj=None, before=None, after=None):
    first, row_parts, tok_parts = plan[:3]
    width = grad.shape[1]
    rows = sum(size for _, size in row_parts)
    tokens = TOK_BLOCK * len(tok_parts)
    in_specs = [HBM] * 4
    out_specs = [HBM, HBM, HBM]
    out_shape = [jax.ShapeDtypeStruct(gate.shape, BF16)] * 2 + [jax.ShapeDtypeStruct((8, 128), F32)]
    if first:
        in_specs.append(HBM)
        out_specs.append(VMEM)
        out_shape.append(jax.ShapeDtypeStruct((2 * proj.shape[0], tokens), BF16))
        extra, aliases = (proj,), {}
    else:
        in_specs += [HBM, HBM, ANY]
        extra, aliases = (*before, after), {4: 0, 5: 1}
    return pl.pallas_call(
        functools.partial(grads_kernel, plan),
        in_specs=in_specs,
        out_specs=out_specs,
        out_shape=out_shape,
        scratch_shapes=[
            pltpu.VMEM((tokens, width), BF16),
            pltpu.VMEM((rows + 64 * first, width), BF16),
            *[pltpu.VMEM((rows, tokens), BF16)] * 4,
            pltpu.VMEM((rows, tokens), F32),
            pltpu.SemaphoreType.DMA((MAX_COPIES,)),
        ],
        input_output_aliases=aliases,
        compiler_params=pltpu.CompilerParams(vmem_limit_bytes=LIMIT),
        cost_estimate=pl.CostEstimate(
            flops=2 * rows * tokens * width,
            bytes_accessed=2 * (tokens + rows) * width + 8 * rows * tokens,
            transcendentals=rows * tokens,
        ),
        name="grads_%d_%d" % (row_parts[0][0], tok_parts[0]),
    )(grad, weight, gate, up, *extra)


def example_kernel(parts_ref, ids_ref, proj_ref, out_ref):
    act = parts_ref[0]
    for part in range(1, 16):
        act = act + parts_ref[part]
    example = lax.broadcasted_iota(jnp.int32, (EXAMPLES, 128), 0)
    members = [ids_ref[block:block + 1, :] == example for block in range(8)]
    projected = proj_ref[...]
    for rank in range(4):
        weighted = jnp.concatenate(
            [
                jnp.where(members[block], act[4 * block + rank:4 * block + rank + 1, :], 0.0)
                for block in range(8)
            ],
            axis=1,
        )
        high = weighted.astype(BF16)
        low = (weighted - high.astype(F32)).astype(BF16)
        first = lax.dot_general(high, projected, NT, preferred_element_type=F32)
        second = lax.dot_general(low, projected[:64], NT, preferred_element_type=F32)
        out_ref[:, 64 * rank:64 * rank + 64] = first[:, :64] + (first[:, 64:] + second)


def example_terms(parts, ids, proj):
    return pl.pallas_call(
        example_kernel,
        out_shape=jax.ShapeDtypeStruct((EXAMPLES, 256), F32),
        compiler_params=pltpu.CompilerParams(vmem_limit_bytes=16 * MIB),
        cost_estimate=pl.CostEstimate(flops=100_000_000, bytes_accessed=700_000, transcendentals=0),
        name="example_terms",
    )(parts, ids, proj)


def score_kernel(terms_ref, queries_ref, out_ref):
    total = terms_ref[0].astype(F32)
    for part in range(1, 8):
        total = total + terms_ref[part].astype(F32)
    scores = lax.dot_general(
        total.astype(BF16), queries_ref[...], NT, preferred_element_type=F32
    )
    for part in range(16):
        for half in range(2):
            out_ref[part, 4 * half:4 * half + 4, :] = scores[
                4 * part:4 * part + 4, 128 * half:128 * half + 128
            ]


def score_parts(terms, queries):
    return pl.pallas_call(
        score_kernel,
        in_specs=[VMEM, VMEM],
        out_specs=VMEM,
        out_shape=jax.ShapeDtypeStruct((16, 8, 128), F32),
        compiler_params=pltpu.CompilerParams(vmem_limit_bytes=16 * MIB),
        cost_estimate=pl.CostEstimate(flops=10_000_000, bytes_accessed=500_000, transcendentals=0),
        name="score_parts",
    )(terms, queries)


def final_kernel(parts_ref, out_ref):
    total = parts_ref[0]
    for part in range(1, 16):
        total = total + parts_ref[part]
    out_ref[:, :128] = total[:4]
    out_ref[:, 128:] = total[4:]


def final_sum(parts):
    return pl.pallas_call(
        final_kernel,
        in_specs=[VMEM],
        out_specs=VMEM,
        out_shape=jax.ShapeDtypeStruct((4, 256), F32),
        compiler_params=pltpu.CompilerParams(vmem_limit_bytes=16 * MIB),
        cost_estimate=pl.CostEstimate(flops=100_000, bytes_accessed=70_000, transcendentals=0),
        name="final_sum",
    )(parts)


def on_device(out_grad, gate_pre, up_pre, down_weight, proj_hidden, proj_out, example_ids, queries):
    gate, up = gate_pre.T, up_pre.T
    exchange = functools.partial(
        lax.all_to_all, axis_name="tensor", split_axis=0, concat_axis=0, tiled=True
    )
    sent = act_parts(gate, up, proj_hidden.T)
    parts = exchange(sent)
    gate_grad, up_grad, _, projected = grads_call(
        FIRST, out_grad, down_weight, gate, up, proj=proj_out.T
    )
    terms = example_terms(parts, example_ids.reshape(8, 128), projected)
    other = lax.ppermute(terms, "dp", [(i, i ^ 1) for i in range(16)])
    pair = (terms + other).astype(BF16)
    pairs = jnp.broadcast_to(pair[None], (8, *pair.shape))
    chips = [[2 * z + core for z in range(8)] for core in range(2)]
    all_terms = lax.all_to_all(
        pairs, "dp", split_axis=0, concat_axis=0, tiled=True, axis_index_groups=chips
    )
    gate_grad, up_grad, order = grads_call(
        SECOND, out_grad, down_weight, gate, up, before=(gate_grad, up_grad), after=pair
    )
    scores = score_parts(all_terms, queries)
    score_terms = exchange(scores)
    gate_grad, up_grad, order = grads_call(
        THIRD, out_grad, down_weight, gate, up, before=(gate_grad, up_grad), after=scores
    )
    return gate_grad.T, up_grad.T, final_sum(score_terms)


def solution(mesh):
    in_specs = (
        P("dp", None),
        P("dp", "tensor"),
        P("dp", "tensor"),
        P("tensor", None),
        P("tensor", None),
        P(),
        P("dp"),
        P("dp", "tensor"),
    )
    out_specs = (P("dp", "tensor"), P("dp", "tensor"), P("tensor", "dp"))
    return jax.shard_map(
        on_device, mesh=mesh, in_specs=in_specs, out_specs=out_specs, check_vma=False
    )
```

```python
import functools
import jax
import jax.numpy as jnp
from jax import lax
from jax.experimental import pallas as pl
from jax.experimental.pallas import tpu as pltpu
from jax.sharding import PartitionSpec as P

F32 = jnp.float32
BF16 = jnp.bfloat16
EXAMPLES = 64
MAX_COPIES = 80
ACT_PARTS = ((0, 256), (256, 256), (512, 176))
LIMIT = 60 << 20
OWN_TOKENS = 64
ROW_PARTS = ((0, 256), (256, 224), (480, 208))
LOADS = (
    ("grad", 0), ("weight", 0), ("grad", 1), ("weight", 1), ("value", 0), ("grad", 2), ("grad", 3),
    ("value", 1), ("weight", 2), ("value", 2),
)
BLOCKS = (
    ((("grad", 0), ("weight", 0)), ((0, 0),), ()),
    ((("grad", 1), ("weight", 1), ("value", 0)), ((0, 1), (1, 0), (1, 1)), ()),
    (
        (("grad", 2), ("grad", 3), ("value", 1)),
        ((0, 2), (1, 2), (0, 3), (1, 3)),
        (0, 1),
    ),
    ((("weight", 2), ("value", 2)), ((2, 0), (2, 1), (2, 2), (2, 3)), (2,)),
)
TOK_BLOCK = 256
NT = (((1,), (1,)), ((), ()))
HBM = pl.BlockSpec(memory_space=pltpu.HBM)
ANY = pl.BlockSpec(memory_space=pl.ANY)
VMEM = pl.BlockSpec(memory_space=pltpu.VMEM)
MIB = 1 << 20


def first_kernel(
    gate_ref, up_ref, act_proj_ref, grad_ref, grad_proj_ref, out_ref,
    gates, ups, act_projs, grads, grad_projs, sems,
):
    own = pl.multiple_of(lax.axis_index("tensor") * OWN_TOKENS, OWN_TOKENS)
    copies = [
        pltpu.make_async_copy(source, target, sems.at[index])
        for index, (source, target) in enumerate((
            (grad_proj_ref, grad_projs),
            (grad_ref.at[pl.ds(own, OWN_TOKENS), :], grads),
            (act_proj_ref, act_projs),
        ))
    ]
    value_copies = []
    for index, (start, rows) in enumerate(ACT_PARTS):
        part = pl.ds(start, rows)
        value_copies.append((
            pltpu.make_async_copy(gate_ref.at[part], gates.at[part], sems.at[3 + 2 * index]),
            pltpu.make_async_copy(up_ref.at[part], ups.at[part], sems.at[4 + 2 * index]),
        ))
    order = [part for pair in value_copies for part in pair]
    for part in order[:2] + copies + order[2:]:
        part.start()
    act = None
    for index, ((gate_copy, up_copy), (start, rows)) in enumerate(zip(value_copies, ACT_PARTS)):
        gate_copy.wait()
        up_copy.wait()
        if index == 0:
            for part in copies:
                part.wait()
            projected = lax.dot_general(
                grads[...], grad_projs[...], NT, preferred_element_type=F32
            )
            half = OWN_TOKENS // 2
            packed = jnp.concatenate([projected[:half], projected[half:]], axis=1).astype(BF16)
            for part in range(16):
                out_ref[part, 32:, :] = packed
        gate = gates[start:start + rows, :].astype(F32)
        up = ups[start:start + rows, :].astype(F32)
        hidden = (gate * jax.nn.sigmoid(gate) * up).astype(BF16)
        term = jnp.dot(act_projs[:, start:start + rows], hidden, preferred_element_type=F32)
        act = term if act is None else act + term
    for part in range(16):
        blocks = [
            act[4 * part:4 * part + 4, 128 * block:128 * block + 128] for block in range(8)
        ]
        out_ref[part, :32, :] = jnp.concatenate(blocks, axis=0).astype(BF16)


def first_parts(gate, up, act_proj, grad, grad_proj):
    hidden_units, tokens = gate.shape
    ranks, width = grad_proj.shape
    return pl.pallas_call(
        first_kernel,
        in_specs=[HBM] * 5,
        out_specs=VMEM,
        out_shape=jax.ShapeDtypeStruct((16, 64, 128), BF16),
        scratch_shapes=[
            pltpu.VMEM(gate.shape, BF16),
            pltpu.VMEM(gate.shape, BF16),
            pltpu.VMEM(act_proj.shape, BF16),
            pltpu.VMEM((OWN_TOKENS, width), BF16),
            pltpu.VMEM(grad_proj.shape, BF16),
            pltpu.SemaphoreType.DMA((3 + 2 * len(ACT_PARTS),)),
        ],
        compiler_params=pltpu.CompilerParams(vmem_limit_bytes=LIMIT),
        cost_estimate=pl.CostEstimate(
            flops=2 * ranks * hidden_units * tokens,
            bytes_accessed=4 * hidden_units * tokens,
            transcendentals=hidden_units * tokens,
        ),
        name="first_parts",
    )(gate, up, act_proj, grad, grad_proj)


def grads_kernel(
    grad_ref, weight_ref, gate_ref, up_ref, _after, gate_out, up_out,
    grads, weights, gates, ups, gate_done, up_done, products, sems,
):
    sem = iter(range(MAX_COPIES))
    copies = {}

    def start(key, *pairs):
        for source, target in pairs:
            part = pltpu.make_async_copy(source, target, sems.at[next(sem)])
            part.start()
            copies.setdefault(key, []).append(part)

    def wait(*keys):
        for key in keys:
            for part in copies.pop(key):
                part.wait()

    def load(kind, part):
        if kind == "grad":
            rows = pl.ds(TOK_BLOCK * part, TOK_BLOCK)
            start((kind, part), (grad_ref.at[rows, :], grads.at[rows, :]))
            return
        rows = pl.ds(*ROW_PARTS[part])
        if kind == "weight":
            start((kind, part), (weight_ref.at[rows, :], weights.at[rows, :]))
        else:
            start(
                (kind, part),
                (gate_ref.at[rows, :], gates.at[rows, :]),
                (up_ref.at[rows, :], ups.at[rows, :]),
            )

    def multiply(row_part, tok_part):
        rows, tok = pl.ds(*ROW_PARTS[row_part]), pl.ds(TOK_BLOCK * tok_part, TOK_BLOCK)
        products[rows, tok] = lax.dot_general(
            weights[rows, :], grads[tok, :], NT, preferred_element_type=F32
        )

    def finish(row_part, tok_part):
        here = (pl.ds(*ROW_PARTS[row_part]), pl.ds(TOK_BLOCK * tok_part, TOK_BLOCK))
        gate = gates[here].astype(F32)
        sig = jax.nn.sigmoid(gate)
        scaled = products[here] * sig
        up_done[here] = (scaled * gate).astype(BF16)
        gate_done[here] = (
            scaled * ups[here].astype(F32) * (1.0 + gate * (1.0 - sig))
        ).astype(BF16)

    def store(row_part):
        rows = pl.ds(*ROW_PARTS[row_part])
        start(
            "out",
            (gate_done.at[rows, :], gate_out.at[rows, :]),
            (up_done.at[rows, :], up_out.at[rows, :]),
        )

    for kind, part in LOADS:
        load(kind, part)
    pending = []
    for needs, tiles, rows_done in BLOCKS:
        wait(*needs)
        for tile in tiles:
            multiply(*tile)
            pending.append(tile)
            while len(pending) > 1 and ("value", pending[0][0]) not in copies:
                finish(*pending.pop(0))
        if rows_done:
            while pending:
                finish(*pending.pop(0))
        for row_part in rows_done:
            store(row_part)
    wait("out")


def grads_call(grad, weight, gate, up, after):
    tokens, width = grad.shape
    rows = gate.shape[0]
    return pl.pallas_call(
        grads_kernel,
        in_specs=[HBM] * 4 + [ANY],
        out_specs=[HBM] * 2,
        out_shape=[jax.ShapeDtypeStruct(gate.shape, BF16)] * 2,
        scratch_shapes=[
            pltpu.VMEM((tokens, width), BF16),
            pltpu.VMEM((rows, width), BF16),
            *[pltpu.VMEM((rows, tokens), BF16)] * 4,
            pltpu.VMEM((rows, tokens), F32),
            pltpu.SemaphoreType.DMA((MAX_COPIES,)),
        ],
        compiler_params=pltpu.CompilerParams(vmem_limit_bytes=LIMIT),
        cost_estimate=pl.CostEstimate(
            flops=2 * rows * tokens * width,
            bytes_accessed=2 * (tokens + rows) * width + 8 * rows * tokens,
            transcendentals=rows * tokens,
        ),
        name="grads",
    )(grad, weight, gate, up, after)


def example_kernel(parts_ref, ids_ref, out_ref):
    act = parts_ref[0, :32, :].astype(F32)
    for part in range(1, 16):
        act = act + parts_ref[part, :32, :].astype(F32)
    projected = []
    for part in range(16):
        packed = parts_ref[part, 32:, :]
        projected += [packed[:, :64], packed[:, 64:]]
    projected = jnp.concatenate(projected, axis=0)
    example = lax.broadcasted_iota(jnp.int32, (EXAMPLES, 128), 0)
    members = [ids_ref[block:block + 1, :] == example for block in range(8)]
    weighted = jnp.concatenate(
        [
            jnp.concatenate(
                [
                    jnp.where(members[block], act[4 * block + rank:4 * block + rank + 1, :], 0.0)
                    for block in range(8)
                ],
                axis=1,
            )
            for rank in range(4)
        ],
        axis=0,
    )
    high = weighted.astype(BF16)
    low = (weighted - high.astype(F32)).astype(BF16)
    terms = jnp.dot(high, projected, preferred_element_type=F32) + jnp.dot(
        low, projected, preferred_element_type=F32
    )
    for rank in range(4):
        out_ref[:, 64 * rank:64 * rank + 64] = terms[EXAMPLES * rank:EXAMPLES * (rank + 1)]


def example_terms(parts, ids):
    return pl.pallas_call(
        example_kernel,
        out_shape=jax.ShapeDtypeStruct((EXAMPLES, 256), F32),
        compiler_params=pltpu.CompilerParams(vmem_limit_bytes=16 * MIB),
        cost_estimate=pl.CostEstimate(flops=100_000_000, bytes_accessed=700_000, transcendentals=0),
        name="example_terms",
    )(parts, ids)


def score_kernel(terms_ref, queries_ref, out_ref):
    total = terms_ref[0].astype(F32)
    for part in range(1, 8):
        total = total + terms_ref[part].astype(F32)
    scores = lax.dot_general(
        total.astype(BF16), queries_ref[...], NT, preferred_element_type=F32
    )
    for part in range(16):
        for half in range(2):
            out_ref[part, 4 * half:4 * half + 4, :] = scores[
                4 * part:4 * part + 4, 128 * half:128 * half + 128
            ]


def score_parts(terms, queries):
    return pl.pallas_call(
        score_kernel,
        in_specs=[VMEM, VMEM],
        out_specs=VMEM,
        out_shape=jax.ShapeDtypeStruct((16, 8, 128), F32),
        compiler_params=pltpu.CompilerParams(vmem_limit_bytes=16 * MIB),
        cost_estimate=pl.CostEstimate(flops=10_000_000, bytes_accessed=500_000, transcendentals=0),
        name="score_parts",
    )(terms, queries)


def final_kernel(parts_ref, out_ref):
    total = parts_ref[0]
    for part in range(1, 16):
        total = total + parts_ref[part]
    out_ref[:, :128] = total[:4]
    out_ref[:, 128:] = total[4:]


def final_sum(parts):
    return pl.pallas_call(
        final_kernel,
        in_specs=[VMEM],
        out_specs=VMEM,
        out_shape=jax.ShapeDtypeStruct((4, 256), F32),
        compiler_params=pltpu.CompilerParams(vmem_limit_bytes=16 * MIB),
        cost_estimate=pl.CostEstimate(flops=100_000, bytes_accessed=70_000, transcendentals=0),
        name="final_sum",
    )(parts)


def on_device(out_grad, gate_pre, up_pre, down_weight, proj_hidden, proj_out, example_ids, queries):
    gate, up = gate_pre.T, up_pre.T
    exchange = functools.partial(
        lax.all_to_all, axis_name="tensor", split_axis=0, concat_axis=0, tiled=True
    )
    parts = exchange(first_parts(gate, up, proj_hidden.T, out_grad, proj_out.T))
    terms = example_terms(parts, example_ids.reshape(8, 128))
    other = lax.ppermute(terms, "dp", [(i, i ^ 1) for i in range(16)])
    pair = (terms + other).astype(BF16)
    pairs = jnp.broadcast_to(pair[None], (8, *pair.shape))
    chips = [[2 * z + core for z in range(8)] for core in range(2)]
    all_terms = lax.all_to_all(
        pairs, "dp", split_axis=0, concat_axis=0, tiled=True, axis_index_groups=chips
    )
    gate_grad, up_grad = grads_call(out_grad, down_weight, gate, up, pair)
    all_terms, gate_grad = lax.optimization_barrier((all_terms, gate_grad))
    score_terms = exchange(score_parts(all_terms, queries))
    return gate_grad.T, up_grad.T, final_sum(score_terms)


def solution(mesh):
    in_specs = (
        P("dp", None),
        P("dp", "tensor"),
        P("dp", "tensor"),
        P("tensor", None),
        P("tensor", None),
        P(),
        P("dp"),
        P("dp", "tensor"),
    )
    out_specs = (P("dp", "tensor"), P("dp", "tensor"), P("tensor", "dp"))
    return jax.shard_map(
        on_device, mesh=mesh, in_specs=in_specs, out_specs=out_specs, check_vma=False
    )
```

```python
import functools
import jax
import jax.numpy as jnp
from jax import lax
from jax.experimental import pallas as pl
from jax.experimental.pallas import tpu as pltpu
from jax.sharding import PartitionSpec as P

F32 = jnp.float32
BF16 = jnp.bfloat16
EXAMPLES = 64
MAX_COPIES = 80
ACT_PARTS = ((0, 128), (128, 256), (384, 256), (640, 48))
LIMIT = 60 << 20
OWN_TOKENS = 64
ROW_PARTS = ((0, 256), (256, 224), (480, 208))
LOADS = (
    ("grad", 0), ("weight", 0), ("grad", 1), ("weight", 1), ("value", 0), ("grad", 2), ("grad", 3),
    ("value", 1), ("weight", 2), ("value", 2),
)
BLOCKS = (
    ((("grad", 0), ("weight", 0)), ((0, 0),), ()),
    ((("grad", 1), ("weight", 1), ("value", 0)), ((0, 1), (1, 0), (1, 1)), ()),
    (
        (("grad", 2), ("grad", 3), ("value", 1)),
        ((0, 2), (1, 2), (0, 3), (1, 3)),
        (0, 1),
    ),
    ((("weight", 2), ("value", 2)), ((2, 0), (2, 1), (2, 2), (2, 3)), (2,)),
)
TOK_BLOCK = 256
NT = (((1,), (1,)), ((), ()))
HBM = pl.BlockSpec(memory_space=pltpu.HBM)
ANY = pl.BlockSpec(memory_space=pl.ANY)
VMEM = pl.BlockSpec(memory_space=pltpu.VMEM)
MIB = 1 << 20


def first_kernel(
    gate_ref, up_ref, act_proj_ref, grad_ref, grad_proj_ref, out_ref,
    gates, ups, act_projs, grads, grad_projs, sems,
):
    own = pl.multiple_of(lax.axis_index("tensor") * OWN_TOKENS, OWN_TOKENS)
    copies = [
        pltpu.make_async_copy(source, target, sems.at[index])
        for index, (source, target) in enumerate((
            (grad_proj_ref, grad_projs),
            (grad_ref.at[pl.ds(own, OWN_TOKENS), :], grads),
            (act_proj_ref, act_projs),
        ))
    ]
    value_copies = []
    for index, (start, rows) in enumerate(ACT_PARTS):
        part = pl.ds(start, rows)
        value_copies.append((
            pltpu.make_async_copy(gate_ref.at[part], gates.at[part], sems.at[3 + 2 * index]),
            pltpu.make_async_copy(up_ref.at[part], ups.at[part], sems.at[4 + 2 * index]),
        ))
    order = [part for pair in value_copies for part in pair]
    for part in copies + order:
        part.start()
    act = None
    for index, ((gate_copy, up_copy), (start, rows)) in enumerate(zip(value_copies, ACT_PARTS)):
        gate_copy.wait()
        up_copy.wait()
        if index == 0:
            for part in copies:
                part.wait()
            projected = lax.dot_general(
                grads[...], grad_projs[...], NT, preferred_element_type=F32
            )
            half = OWN_TOKENS // 2
            packed = jnp.concatenate([projected[:half], projected[half:]], axis=1).astype(BF16)
            for part in range(16):
                out_ref[part, 32:, :] = packed
        gate = gates[start:start + rows, :].astype(F32)
        up = ups[start:start + rows, :].astype(F32)
        hidden = (gate * jax.nn.sigmoid(gate) * up).astype(BF16)
        term = jnp.dot(act_projs[:, start:start + rows], hidden, preferred_element_type=F32)
        act = term if act is None else act + term
    for part in range(16):
        blocks = [
            act[4 * part:4 * part + 4, 128 * block:128 * block + 128] for block in range(8)
        ]
        out_ref[part, :32, :] = jnp.concatenate(blocks, axis=0).astype(BF16)


def first_parts(gate, up, act_proj, grad, grad_proj):
    hidden_units, tokens = gate.shape
    ranks, width = grad_proj.shape
    return pl.pallas_call(
        first_kernel,
        in_specs=[HBM] * 5,
        out_specs=VMEM,
        out_shape=jax.ShapeDtypeStruct((16, 64, 128), BF16),
        scratch_shapes=[
            pltpu.VMEM(gate.shape, BF16),
            pltpu.VMEM(gate.shape, BF16),
            pltpu.VMEM(act_proj.shape, BF16),
            pltpu.VMEM((OWN_TOKENS, width), BF16),
            pltpu.VMEM(grad_proj.shape, BF16),
            pltpu.SemaphoreType.DMA((3 + 2 * len(ACT_PARTS),)),
        ],
        compiler_params=pltpu.CompilerParams(vmem_limit_bytes=LIMIT),
        cost_estimate=pl.CostEstimate(
            flops=2 * ranks * hidden_units * tokens,
            bytes_accessed=4 * hidden_units * tokens,
            transcendentals=hidden_units * tokens,
        ),
        name="first_parts",
    )(gate, up, act_proj, grad, grad_proj)


def grads_kernel(
    grad_ref, weight_ref, gate_ref, up_ref, _after, gate_out, up_out,
    grads, weights, gates, ups, gate_done, up_done, products, sems,
):
    sem = iter(range(MAX_COPIES))
    copies = {}

    def start(key, *pairs):
        for source, target in pairs:
            part = pltpu.make_async_copy(source, target, sems.at[next(sem)])
            part.start()
            copies.setdefault(key, []).append(part)

    def wait(*keys):
        for key in keys:
            for part in copies.pop(key):
                part.wait()

    def load(kind, part):
        if kind == "grad":
            rows = pl.ds(TOK_BLOCK * part, TOK_BLOCK)
            start((kind, part), (grad_ref.at[rows, :], grads.at[rows, :]))
            return
        rows = pl.ds(*ROW_PARTS[part])
        if kind == "weight":
            start((kind, part), (weight_ref.at[rows, :], weights.at[rows, :]))
        else:
            start(
                (kind, part),
                (gate_ref.at[rows, :], gates.at[rows, :]),
                (up_ref.at[rows, :], ups.at[rows, :]),
            )

    def multiply(row_part, tok_part):
        rows, tok = pl.ds(*ROW_PARTS[row_part]), pl.ds(TOK_BLOCK * tok_part, TOK_BLOCK)
        products[rows, tok] = lax.dot_general(
            weights[rows, :], grads[tok, :], NT, preferred_element_type=F32
        )

    def finish(row_part, tok_part):
        here = (pl.ds(*ROW_PARTS[row_part]), pl.ds(TOK_BLOCK * tok_part, TOK_BLOCK))
        gate = gates[here].astype(F32)
        sig = jax.nn.sigmoid(gate)
        scaled = products[here] * sig
        up_done[here] = (scaled * gate).astype(BF16)
        gate_done[here] = (
            scaled * ups[here].astype(F32) * (1.0 + gate * (1.0 - sig))
        ).astype(BF16)

    def store(row_part):
        rows = pl.ds(*ROW_PARTS[row_part])
        start(
            "out",
            (gate_done.at[rows, :], gate_out.at[rows, :]),
            (up_done.at[rows, :], up_out.at[rows, :]),
        )

    for kind, part in LOADS:
        load(kind, part)
    pending = []
    for needs, tiles, rows_done in BLOCKS:
        wait(*needs)
        for tile in tiles:
            multiply(*tile)
            pending.append(tile)
            while len(pending) > 1 and ("value", pending[0][0]) not in copies:
                finish(*pending.pop(0))
        if rows_done:
            while pending:
                finish(*pending.pop(0))
        for row_part in rows_done:
            store(row_part)
    wait("out")


def grads_call(grad, weight, gate, up, after):
    tokens, width = grad.shape
    rows = gate.shape[0]
    return pl.pallas_call(
        grads_kernel,
        in_specs=[HBM] * 4 + [ANY],
        out_specs=[HBM] * 2,
        out_shape=[jax.ShapeDtypeStruct(gate.shape, BF16)] * 2,
        scratch_shapes=[
            pltpu.VMEM((tokens, width), BF16),
            pltpu.VMEM((rows, width), BF16),
            *[pltpu.VMEM((rows, tokens), BF16)] * 4,
            pltpu.VMEM((rows, tokens), F32),
            pltpu.SemaphoreType.DMA((MAX_COPIES,)),
        ],
        compiler_params=pltpu.CompilerParams(vmem_limit_bytes=LIMIT),
        cost_estimate=pl.CostEstimate(
            flops=2 * rows * tokens * width,
            bytes_accessed=2 * (tokens + rows) * width + 8 * rows * tokens,
            transcendentals=rows * tokens,
        ),
        name="grads",
    )(grad, weight, gate, up, after)


def example_kernel(parts_ref, ids_ref, out_ref):
    act = parts_ref[0, :32, :].astype(F32)
    for part in range(1, 16):
        act = act + parts_ref[part, :32, :].astype(F32)
    projected = []
    for part in range(16):
        packed = parts_ref[part, 32:, :]
        projected += [packed[:, :64], packed[:, 64:]]
    projected = jnp.concatenate(projected, axis=0)
    example = lax.broadcasted_iota(jnp.int32, (EXAMPLES, 128), 0)
    members = [ids_ref[block:block + 1, :] == example for block in range(8)]
    weighted = jnp.concatenate(
        [
            jnp.concatenate(
                [
                    jnp.where(members[block], act[4 * block + rank:4 * block + rank + 1, :], 0.0)
                    for block in range(8)
                ],
                axis=1,
            )
            for rank in range(4)
        ],
        axis=0,
    )
    high = weighted.astype(BF16)
    low = (weighted - high.astype(F32)).astype(BF16)
    terms = jnp.dot(high, projected, preferred_element_type=F32) + jnp.dot(
        low, projected, preferred_element_type=F32
    )
    for rank in range(4):
        out_ref[:, 64 * rank:64 * rank + 64] = terms[EXAMPLES * rank:EXAMPLES * (rank + 1)]


def example_terms(parts, ids):
    return pl.pallas_call(
        example_kernel,
        out_shape=jax.ShapeDtypeStruct((EXAMPLES, 256), F32),
        compiler_params=pltpu.CompilerParams(vmem_limit_bytes=16 * MIB),
        cost_estimate=pl.CostEstimate(flops=100_000_000, bytes_accessed=700_000, transcendentals=0),
        name="example_terms",
    )(parts, ids)


def score_kernel(terms_ref, queries_ref, out_ref):
    total = terms_ref[0].astype(F32)
    for part in range(1, 8):
        total = total + terms_ref[part].astype(F32)
    scores = lax.dot_general(
        total.astype(BF16), queries_ref[...], NT, preferred_element_type=F32
    )
    for part in range(16):
        for half in range(2):
            out_ref[part, 4 * half:4 * half + 4, :] = scores[
                4 * part:4 * part + 4, 128 * half:128 * half + 128
            ]


def score_parts(terms, queries):
    return pl.pallas_call(
        score_kernel,
        in_specs=[VMEM, VMEM],
        out_specs=VMEM,
        out_shape=jax.ShapeDtypeStruct((16, 8, 128), F32),
        compiler_params=pltpu.CompilerParams(vmem_limit_bytes=16 * MIB),
        cost_estimate=pl.CostEstimate(flops=10_000_000, bytes_accessed=500_000, transcendentals=0),
        name="score_parts",
    )(terms, queries)


def final_kernel(parts_ref, out_ref):
    total = parts_ref[0]
    for part in range(1, 16):
        total = total + parts_ref[part]
    out_ref[:, :128] = total[:4]
    out_ref[:, 128:] = total[4:]


def final_sum(parts):
    return pl.pallas_call(
        final_kernel,
        in_specs=[VMEM],
        out_specs=VMEM,
        out_shape=jax.ShapeDtypeStruct((4, 256), F32),
        compiler_params=pltpu.CompilerParams(vmem_limit_bytes=16 * MIB),
        cost_estimate=pl.CostEstimate(flops=100_000, bytes_accessed=70_000, transcendentals=0),
        name="final_sum",
    )(parts)


def on_device(out_grad, gate_pre, up_pre, down_weight, proj_hidden, proj_out, example_ids, queries):
    gate, up = gate_pre.T, up_pre.T
    exchange = functools.partial(
        lax.all_to_all, axis_name="tensor", split_axis=0, concat_axis=0, tiled=True
    )
    parts = exchange(first_parts(gate, up, proj_hidden.T, out_grad, proj_out.T))
    terms = example_terms(parts, example_ids.reshape(8, 128))
    other = lax.ppermute(terms, "dp", [(i, i ^ 1) for i in range(16)])
    pair = (terms + other).astype(BF16)
    pairs = jnp.broadcast_to(pair[None], (8, *pair.shape))
    chips = [[2 * z + core for z in range(8)] for core in range(2)]
    all_terms = lax.all_to_all(
        pairs, "dp", split_axis=0, concat_axis=0, tiled=True, axis_index_groups=chips
    )
    gate_grad, up_grad = grads_call(out_grad, down_weight, gate, up, pair)
    all_terms, gate_grad = lax.optimization_barrier((all_terms, gate_grad))
    score_terms = exchange(score_parts(all_terms, queries))
    return gate_grad.T, up_grad.T, final_sum(score_terms)


def solution(mesh):
    in_specs = (
        P("dp", None),
        P("dp", "tensor"),
        P("dp", "tensor"),
        P("tensor", None),
        P("tensor", None),
        P(),
        P("dp"),
        P("dp", "tensor"),
    )
    out_specs = (P("dp", "tensor"), P("dp", "tensor"), P("tensor", "dp"))
    return jax.shard_map(
        on_device, mesh=mesh, in_specs=in_specs, out_specs=out_specs, check_vma=False
    )
```

```python
import functools
import jax
import jax.numpy as jnp
from jax import lax
from jax.experimental import pallas as pl
from jax.experimental.pallas import tpu as pltpu
from jax.sharding import PartitionSpec as P

F32 = jnp.float32
BF16 = jnp.bfloat16
EXAMPLES = 64
MAX_COPIES = 80
ACT_PARTS = ((0, 128), (128, 256), (384, 256), (640, 48))
LIMIT = 60 << 20
OWN_TOKENS = 64
ROW_PARTS = ((0, 256), (256, 224), (480, 208))
LOADS = (
    ("grad", 0), ("weight", 0), ("grad", 1), ("weight", 1), ("value", 0), ("grad", 2), ("grad", 3),
    ("value", 1), ("weight", 2), ("value", 2),
)
BLOCKS = (
    ((("grad", 0), ("weight", 0)), ((0, 0),), ()),
    ((("grad", 1), ("weight", 1), ("value", 0)), ((0, 1), (1, 0), (1, 1)), ()),
    (
        (("grad", 2), ("grad", 3), ("value", 1)),
        ((0, 2), (1, 2), (0, 3), (1, 3)),
        (0, 1),
    ),
    ((("weight", 2), ("value", 2)), ((2, 0), (2, 1), (2, 2), (2, 3)), (2,)),
)
TOK_BLOCK = 256
NT = (((1,), (1,)), ((), ()))
HBM = pl.BlockSpec(memory_space=pltpu.HBM)
ANY = pl.BlockSpec(memory_space=pl.ANY)
VMEM = pl.BlockSpec(memory_space=pltpu.VMEM)
MIB = 1 << 20


def first_kernel(
    gate_ref, up_ref, act_proj_ref, grad_ref, grad_proj_ref, out_ref,
    gates, ups, act_projs, grads, grad_projs, sems,
):
    own = pl.multiple_of(lax.axis_index("tensor") * OWN_TOKENS, OWN_TOKENS)
    copies = [
        pltpu.make_async_copy(source, target, sems.at[index])
        for index, (source, target) in enumerate((
            (grad_proj_ref, grad_projs),
            (grad_ref.at[pl.ds(own, OWN_TOKENS), :], grads),
            (act_proj_ref, act_projs),
        ))
    ]
    value_copies = []
    for index, (start, rows) in enumerate(ACT_PARTS):
        part = pl.ds(start, rows)
        value_copies.append((
            pltpu.make_async_copy(gate_ref.at[part], gates.at[part], sems.at[3 + 2 * index]),
            pltpu.make_async_copy(up_ref.at[part], ups.at[part], sems.at[4 + 2 * index]),
        ))
    order = [part for pair in value_copies for part in pair]
    for part in copies + order:
        part.start()
    act = None
    for index, ((gate_copy, up_copy), (start, rows)) in enumerate(zip(value_copies, ACT_PARTS)):
        gate_copy.wait()
        up_copy.wait()
        if index == 0:
            for part in copies:
                part.wait()
            projected = lax.dot_general(
                grads[...], grad_projs[...], NT, preferred_element_type=F32
            )
            half = OWN_TOKENS // 2
            packed = jnp.concatenate([projected[:half], projected[half:]], axis=1).astype(BF16)
            for part in range(16):
                out_ref[part, 32:, :] = packed
        gate = gates[start:start + rows, :].astype(F32)
        up = ups[start:start + rows, :].astype(F32)
        hidden = (gate * jax.nn.sigmoid(gate) * up).astype(BF16)
        term = jnp.dot(act_projs[:, start:start + rows], hidden, preferred_element_type=F32)
        act = term if act is None else act + term
    for part in range(16):
        blocks = [
            act[4 * part:4 * part + 4, 128 * block:128 * block + 128] for block in range(8)
        ]
        out_ref[part, :32, :] = jnp.concatenate(blocks, axis=0).astype(BF16)


def first_parts(gate, up, act_proj, grad, grad_proj):
    hidden_units, tokens = gate.shape
    ranks, width = grad_proj.shape
    return pl.pallas_call(
        first_kernel,
        in_specs=[HBM] * 5,
        out_specs=VMEM,
        out_shape=jax.ShapeDtypeStruct((16, 64, 128), BF16),
        scratch_shapes=[
            pltpu.VMEM(gate.shape, BF16),
            pltpu.VMEM(gate.shape, BF16),
            pltpu.VMEM(act_proj.shape, BF16),
            pltpu.VMEM((OWN_TOKENS, width), BF16),
            pltpu.VMEM(grad_proj.shape, BF16),
            pltpu.SemaphoreType.DMA((3 + 2 * len(ACT_PARTS),)),
        ],
        compiler_params=pltpu.CompilerParams(vmem_limit_bytes=LIMIT),
        cost_estimate=pl.CostEstimate(
            flops=2 * ranks * hidden_units * tokens,
            bytes_accessed=4 * hidden_units * tokens,
            transcendentals=hidden_units * tokens,
        ),
        name="first_parts",
    )(gate, up, act_proj, grad, grad_proj)


def grads_kernel(
    grad_ref, weight_ref, gate_ref, up_ref, _after, gate_out, up_out,
    grads, weights, gates, ups, gate_done, up_done, products, sems,
):
    sem = iter(range(MAX_COPIES))
    copies = {}

    def start(key, *pairs):
        for source, target in pairs:
            part = pltpu.make_async_copy(source, target, sems.at[next(sem)])
            part.start()
            copies.setdefault(key, []).append(part)

    def wait(*keys):
        for key in keys:
            for part in copies.pop(key):
                part.wait()

    def load(kind, part):
        if kind == "grad":
            rows = pl.ds(TOK_BLOCK * part, TOK_BLOCK)
            start((kind, part), (grad_ref.at[rows, :], grads.at[rows, :]))
            return
        rows = pl.ds(*ROW_PARTS[part])
        if kind == "weight":
            start((kind, part), (weight_ref.at[rows, :], weights.at[rows, :]))
        else:
            start(
                (kind, part),
                (gate_ref.at[rows, :], gates.at[rows, :]),
                (up_ref.at[rows, :], ups.at[rows, :]),
            )

    def multiply(row_part, tok_part):
        rows, tok = pl.ds(*ROW_PARTS[row_part]), pl.ds(TOK_BLOCK * tok_part, TOK_BLOCK)
        row, size = ROW_PARTS[row_part]
        lead = 256 - size
        product = lax.dot_general(
            weights[pl.ds(row - lead, 256), :], grads[tok, :], NT, preferred_element_type=F32
        )
        products[rows, tok] = product[lead:]

    def finish(row_part, tok_part):
        here = (pl.ds(*ROW_PARTS[row_part]), pl.ds(TOK_BLOCK * tok_part, TOK_BLOCK))
        gate = gates[here].astype(F32)
        sig = jax.nn.sigmoid(gate)
        scaled = products[here] * sig
        up_done[here] = (scaled * gate).astype(BF16)
        gate_done[here] = (
            scaled * ups[here].astype(F32) * (1.0 + gate * (1.0 - sig))
        ).astype(BF16)

    def store(row_part):
        rows = pl.ds(*ROW_PARTS[row_part])
        start(
            "out",
            (gate_done.at[rows, :], gate_out.at[rows, :]),
            (up_done.at[rows, :], up_out.at[rows, :]),
        )

    for kind, part in LOADS:
        load(kind, part)
    pending = []
    for needs, tiles, rows_done in BLOCKS:
        wait(*needs)
        for tile in tiles:
            multiply(*tile)
            pending.append(tile)
            while len(pending) > 1 and ("value", pending[0][0]) not in copies:
                finish(*pending.pop(0))
        if rows_done:
            while pending:
                finish(*pending.pop(0))
        for row_part in rows_done:
            store(row_part)
    wait("out")


def grads_call(grad, weight, gate, up, after):
    tokens, width = grad.shape
    rows = gate.shape[0]
    return pl.pallas_call(
        grads_kernel,
        in_specs=[HBM] * 4 + [ANY],
        out_specs=[HBM] * 2,
        out_shape=[jax.ShapeDtypeStruct(gate.shape, BF16)] * 2,
        scratch_shapes=[
            pltpu.VMEM((tokens, width), BF16),
            pltpu.VMEM((rows, width), BF16),
            *[pltpu.VMEM((rows, tokens), BF16)] * 4,
            pltpu.VMEM((rows, tokens), F32),
            pltpu.SemaphoreType.DMA((MAX_COPIES,)),
        ],
        compiler_params=pltpu.CompilerParams(vmem_limit_bytes=LIMIT),
        cost_estimate=pl.CostEstimate(
            flops=2 * rows * tokens * width,
            bytes_accessed=2 * (tokens + rows) * width + 8 * rows * tokens,
            transcendentals=rows * tokens,
        ),
        name="grads",
    )(grad, weight, gate, up, after)


def example_kernel(parts_ref, ids_ref, out_ref):
    act = parts_ref[0, :32, :].astype(F32)
    for part in range(1, 16):
        act = act + parts_ref[part, :32, :].astype(F32)
    projected = []
    for part in range(16):
        packed = parts_ref[part, 32:, :]
        projected += [packed[:, :64], packed[:, 64:]]
    projected = jnp.concatenate(projected, axis=0)
    example = lax.broadcasted_iota(jnp.int32, (EXAMPLES, 128), 0)
    members = [ids_ref[block:block + 1, :] == example for block in range(8)]
    weighted = jnp.concatenate(
        [
            jnp.concatenate(
                [
                    jnp.where(members[block], act[4 * block + rank:4 * block + rank + 1, :], 0.0)
                    for block in range(8)
                ],
                axis=1,
            )
            for rank in range(4)
        ],
        axis=0,
    )
    high = weighted.astype(BF16)
    low = (weighted - high.astype(F32)).astype(BF16)
    terms = jnp.dot(high, projected, preferred_element_type=F32) + jnp.dot(
        low, projected, preferred_element_type=F32
    )
    for rank in range(4):
        out_ref[:, 64 * rank:64 * rank + 64] = terms[EXAMPLES * rank:EXAMPLES * (rank + 1)]


def example_terms(parts, ids):
    return pl.pallas_call(
        example_kernel,
        out_shape=jax.ShapeDtypeStruct((EXAMPLES, 256), F32),
        compiler_params=pltpu.CompilerParams(vmem_limit_bytes=16 * MIB),
        cost_estimate=pl.CostEstimate(flops=100_000_000, bytes_accessed=700_000, transcendentals=0),
        name="example_terms",
    )(parts, ids)


def score_kernel(terms_ref, queries_ref, out_ref):
    total = terms_ref[0].astype(F32)
    for part in range(1, 8):
        total = total + terms_ref[part].astype(F32)
    scores = lax.dot_general(
        total.astype(BF16), queries_ref[...], NT, preferred_element_type=F32
    )
    for part in range(16):
        for half in range(2):
            out_ref[part, 4 * half:4 * half + 4, :] = scores[
                4 * part:4 * part + 4, 128 * half:128 * half + 128
            ]


def score_parts(terms, queries):
    return pl.pallas_call(
        score_kernel,
        in_specs=[VMEM, VMEM],
        out_specs=VMEM,
        out_shape=jax.ShapeDtypeStruct((16, 8, 128), F32),
        compiler_params=pltpu.CompilerParams(vmem_limit_bytes=16 * MIB),
        cost_estimate=pl.CostEstimate(flops=10_000_000, bytes_accessed=500_000, transcendentals=0),
        name="score_parts",
    )(terms, queries)


def final_kernel(parts_ref, out_ref):
    total = parts_ref[0]
    for part in range(1, 16):
        total = total + parts_ref[part]
    out_ref[:, :128] = total[:4]
    out_ref[:, 128:] = total[4:]


def final_sum(parts):
    return pl.pallas_call(
        final_kernel,
        in_specs=[VMEM],
        out_specs=VMEM,
        out_shape=jax.ShapeDtypeStruct((4, 256), F32),
        compiler_params=pltpu.CompilerParams(vmem_limit_bytes=16 * MIB),
        cost_estimate=pl.CostEstimate(flops=100_000, bytes_accessed=70_000, transcendentals=0),
        name="final_sum",
    )(parts)


def on_device(out_grad, gate_pre, up_pre, down_weight, proj_hidden, proj_out, example_ids, queries):
    gate, up = gate_pre.T, up_pre.T
    exchange = functools.partial(
        lax.all_to_all, axis_name="tensor", split_axis=0, concat_axis=0, tiled=True
    )
    parts = exchange(first_parts(gate, up, proj_hidden.T, out_grad, proj_out.T))
    terms = example_terms(parts, example_ids.reshape(8, 128))
    other = lax.ppermute(terms, "dp", [(i, i ^ 1) for i in range(16)])
    pair = (terms + other).astype(BF16)
    pairs = jnp.broadcast_to(pair[None], (8, *pair.shape))
    chips = [[2 * z + core for z in range(8)] for core in range(2)]
    all_terms = lax.all_to_all(
        pairs, "dp", split_axis=0, concat_axis=0, tiled=True, axis_index_groups=chips
    )
    gate_grad, up_grad = grads_call(out_grad, down_weight, gate, up, pair)
    all_terms, gate_grad = lax.optimization_barrier((all_terms, gate_grad))
    score_terms = exchange(score_parts(all_terms, queries))
    return gate_grad.T, up_grad.T, final_sum(score_terms)


def solution(mesh):
    in_specs = (
        P("dp", None),
        P("dp", "tensor"),
        P("dp", "tensor"),
        P("tensor", None),
        P("tensor", None),
        P(),
        P("dp"),
        P("dp", "tensor"),
    )
    out_specs = (P("dp", "tensor"), P("dp", "tensor"), P("tensor", "dp"))
    return jax.shard_map(
        on_device, mesh=mesh, in_specs=in_specs, out_specs=out_specs, check_vma=False
    )
```
